512 devices in a mesh: mesh: 128 (over y, z, core), sub: 4 (over x).
Axes of the slice: x: 4, y: 8, z: 8, core: 2. Of those that a mesh axis runs over, the one named last changes fastest.
Arguments:
- disp: float32 [3, 2097152], P(None, ('mesh', 'sub')), may hold values from -6 to 6
- velo: float32 [3, 2097152], P(None, ('mesh', 'sub')), may hold values from -6 to 6
- inv_mass: float32 [2097152], P(('mesh', 'sub')), may hold values from 0.05 to 0.2
- hex_nodes: int32 [8, 1048576], P(None, ('mesh', 'sub')), may hold values from -1024 to 5119, as said below
- modulus: float32 [1048576], P(('mesh', 'sub')), may hold values from 0.5 to 2
- yielded: int32 [1048576], P(('mesh', 'sub')), may hold values 0 or 1
- stiffness: float32 [24, 24], replicated
- send_slots: int32 [65536, 32], P(('mesh', 'sub')), may hold values from 0 to 4095, as said below
- fine_slot: int32 [2097152], P(('mesh', 'sub')), may hold values from 0 to 4095, as said below
- fine_disp: float32 [3, 2097152], P(None, ('mesh', 'sub')), may hold values from -6 to 6
- fine_velo: float32 [3, 2097152], P(None, ('mesh', 'sub')), may hold values from -6 to 6
- fine_inv_mass: float32 [2097152], P(('mesh', 'sub')), may hold values from 0.5 to 2
- fine_stiff: float32 [2097152], P(('mesh', 'sub')), may hold values from 0.25 to 1
- tie_stiff: float32 [2097152], P(('mesh', 'sub')), may hold values from 0.25 to 1
Outputs:
- disp_new: float32 [3, 2097152], P(None, ('mesh', 'sub'))
- velo_new: float32 [3, 2097152], P(None, ('mesh', 'sub'))
- fine_pos: float32 [3, 2097152], P(None, ('mesh', 'sub'))
- fine_vel: float32 [3, 2097152], P(None, ('mesh', 'sub'))
The draws below stay inside these ranges and needn't reach their ends.
Inputs may be any that keep to these rules, and one draw needn't show every extreme that they name: `hex_nodes`: each offset names a node among the device's 4096 nodes or the 1024 nodes on either side of them, and always a node of the whole mesh. `send_slots`: every slot holds a local node number of its owner. `fine_slot`: each helper's 4096 entries are a permutation of 0 to 4095.
All inputs are finite; a program needn't handle non-finite values. No bound on the sum of `yielded` on one device may be relied on, other than what follows from the above.
Results may differ from the reference program's by a relative error of at most 0.00027.
Values sent between devices are 32-bit elements; how exact they have to be, the bound alone decides.
A program may use at most 64 MiB of HBM per device.

```python
import math
import jax
import jax.numpy as jnp
from jax import lax

NN_DEV = 4096
NE_DEV = 2048
CAP = 32
SUBSTEPS = 8
GHOST = 1024
NF_DEV = 4096
NN = 2097152
NE = 1048576
NF = 2097152
N_MESH = 128
N_SUB = 4
DEVICES = 512


def draw_hex_nodes(key, part):
    key = jax.random.fold_in(key, 11)
    offset = jax.random.randint(key, (8, NE), -GHOST, NN_DEV + GHOST)
    device = jnp.arange(NE, dtype=jnp.int32)[None, :] // NE_DEV
    offset = offset.at[0, NE_DEV].set(-GHOST)
    offset = offset.at[1, NE_DEV].set(NN_DEV + GHOST - 1)
    global_nodes = jnp.clip(device * NN_DEV + offset, 0, NN - 1)
    return (global_nodes - device * NN_DEV).astype(jnp.int32)


def draw_stiffness(key, part):
    key = jax.random.fold_in(key, 12)
    key_off, key_diag = jax.random.split(key)
    offdiag = jax.random.uniform(key_off, (24, 24), jnp.float32, -0.04, 0.04)
    diagonal = jax.random.uniform(key_diag, (24,), jnp.float32, 1.0, 1.5)
    eye = jnp.eye(24, dtype=jnp.float32)
    return offdiag * (1.0 - eye) + eye * diagonal[None, :]


def draw_send_slots(key, part):
    key = jax.random.fold_in(key, 13)
    values = jax.random.randint(key, (DEVICES * N_MESH, CAP), 0, NN_DEV)
    values = values.at[0, 0].set(0)
    values = values.at[0, CAP - 1].set(NN_DEV - 1)
    return values.astype(jnp.int32)


def draw_fine_slot(key, part):
    key = jax.random.fold_in(key, 14)
    keys = jax.random.split(key, DEVICES)
    table = jax.vmap(lambda single: jax.random.permutation(single, NF_DEV))(keys)
    return table.reshape(NF).astype(jnp.int32)


def with_ends(entries, stream_key, smallest, high):
    dims = entries.shape
    spot = [jax.random.randint(jax.random.fold_in(stream_key, axis), (), 0, dims[axis]) for axis in range(len(dims))]
    entries = entries.at[tuple(spot)].set(smallest)
    longest = dims.index(max(dims))
    spot[longest] = (spot[longest] + 1) % dims[longest]
    return entries.at[tuple(spot)].set(high)


def block_scale(own_key, extent, shards, smallest, largest):
    gain, own = 1.0, jax.random.fold_in(own_key, 6)
    for axis_at, shards_of in shards:
        steps = jnp.exp(jax.random.uniform(jax.random.fold_in(own, axis_at), (shards_of,), jnp.float32, smallest / len(shards), largest / len(shards)))
        gain = gain * jnp.repeat(steps, extent[axis_at] // shards_of).reshape([-1 if axis == axis_at else 1 for axis in range(len(extent))])
    return gain


def centred(stream_key, dims, deviation, most, cuts=(), kind=jnp.bfloat16):
    entries = deviation * jax.random.normal(stream_key, dims, jnp.float32)
    if cuts:
        entries = entries * block_scale(stream_key, dims, cuts, -0.22, 0.18)
    return jnp.clip(entries, -most, most).astype(kind)


def setup_inputs(seed: int = 0) -> dict:
    streams_of = jax.random.split(jax.random.key(seed), 15)
    return {
        "disp": centred(streams_of[0], (3, NN), 1.0, 6.0, ((1, 512),), jnp.float32),
        "velo": centred(streams_of[1], (3, NN), 1.0, 6.0, ((1, 512),), jnp.float32),
        "inv_mass": jnp.clip(jnp.exp(math.log(0.2) - 1.3862944 * jax.random.uniform(streams_of[2], (NN,), jnp.float32) ** block_scale(streams_of[2], (NN,), ((0, 512),), -0.2, 0.2)), 0.05, 0.2),
        "hex_nodes": draw_hex_nodes(jax.random.fold_in(streams_of[14], 71), 0),
        "modulus": jnp.clip(jnp.exp(math.log(2.0) - 1.3862944 * jax.random.uniform(streams_of[4], (NE,), jnp.float32) ** block_scale(streams_of[4], (NE,), ((0, 512),), -0.2, 0.2)), 0.5, 2.0),
        "yielded": with_ends((jax.random.randint(streams_of[5], (NE,), 0, 3) < 1).astype(jnp.int32), jax.random.fold_in(streams_of[5], 1), 0, 1),
        "stiffness": draw_stiffness(jax.random.fold_in(streams_of[14], 71), 0),
        "send_slots": draw_send_slots(jax.random.fold_in(streams_of[14], 71), 0),
        "fine_slot": draw_fine_slot(jax.random.fold_in(streams_of[14], 71), 0),
        "fine_disp": centred(streams_of[9], (3, NF), 1.0, 6.0, ((1, 512),), jnp.float32),
        "fine_velo": centred(streams_of[10], (3, NF), 1.0, 6.0, ((1, 512),), jnp.float32),
        "fine_inv_mass": jnp.clip(jnp.exp(math.log(2.0) - 1.3862944 * jax.random.uniform(streams_of[11], (NF,), jnp.float32) ** block_scale(streams_of[11], (NF,), ((0, 512),), -0.2, 0.2)), 0.5, 2.0),
        "fine_stiff": jnp.clip(jnp.exp(math.log(1.0) - 1.3862944 * jax.random.uniform(streams_of[12], (NF,), jnp.float32) ** block_scale(streams_of[12], (NF,), ((0, 512),), -0.2, 0.2)), 0.25, 1.0),
        "tie_stiff": jnp.clip(jnp.exp(math.log(1.0) - 1.3862944 * jax.random.uniform(streams_of[13], (NF,), jnp.float32) ** block_scale(streams_of[13], (NF,), ((0, 512),), -0.2, 0.2)), 0.25, 1.0),
    }


DT_FINE = 0.5
DT_COARSE = 1.0
PLASTIC = 0.3


def reference(disp, velo, inv_mass, hex_nodes, modulus, yielded, stiffness, send_slots, fine_slot, fine_disp, fine_velo, fine_inv_mass, fine_stiff, tie_stiff):
    block = (jnp.arange(NE, dtype=jnp.int32) // NE_DEV)[None, :]
    global_nodes = (block * NN_DEV + hex_nodes).astype(jnp.int32)
    corner = disp[:, global_nodes].reshape(24, NE)
    factor = modulus * jnp.where(yielded == 1, PLASTIC, 1.0)
    element = (jnp.dot(stiffness, corner, precision=lax.Precision.HIGHEST) * factor).reshape(3, 8, NE)
    internal = jnp.zeros((3, NN), jnp.float32).at[:, global_nodes].add(element)
    helper = jnp.arange(DEVICES, dtype=jnp.int32)[:, None]
    slot_table = send_slots.reshape(DEVICES, N_MESH, CAP)
    slots = fine_slot.reshape(DEVICES, NF_DEV)
    owner = (slots // CAP) * N_SUB + helper % N_SUB
    local_node = slot_table[owner, helper // N_SUB, slots % CAP]
    target = (owner * NN_DEV + local_node).reshape(NF).astype(jnp.int32)
    attached = disp[:, target]
    fine_pos = fine_disp
    fine_vel = fine_velo
    total = jnp.zeros((3, NF), jnp.float32)
    for substep in range(SUBSTEPS):
        padded = jnp.pad(fine_pos, ((0, 0), (1, 1)))
        laplace = padded[:, 2:] - 2.0 * fine_pos + padded[:, :-2]
        accel = fine_inv_mass * (fine_stiff * laplace + tie_stiff * (attached - fine_pos))
        fine_vel = fine_vel + DT_FINE * accel
        fine_pos = fine_pos + DT_FINE * fine_vel
        total = total + fine_pos
    tie_force = tie_stiff * (total * (1.0 / SUBSTEPS) - attached)
    coupling = jnp.zeros((3, NN), jnp.float32).at[:, target].add(tie_force)
    velo_new = velo + DT_COARSE * (inv_mass * (coupling - internal))
    disp_new = disp + DT_COARSE * velo_new
    return disp_new, velo_new, fine_pos, fine_vel
```

```python
import jax
import jax.numpy as jnp
from jax import lax
from jax.experimental import pallas as pl
from jax.experimental.pallas import tpu as pltpu
from jax.sharding import PartitionSpec as P

SUBSTEPS = 8
DT_FINE = 0.5
DT_COARSE = 1.0
PLASTIC = 0.3

LANES = 128
CAP = 32
PEERS = 128
GROUPS = LANES // CAP
ROWS = 32
RIM = 8
EXT = ROWS + 2 * RIM
ELEMS = 2048
CHUNK = 512
EDGE = 8
MESH = pl.DeviceIdType.MESH
F32 = jnp.float32
BF16 = jnp.bfloat16


def lane_lookup(acc, table_row, rows, row_idx, lane_idx):
    acc = list(acc)
    for r in rows:
        hit = row_idx == r
        for c in range(3):
            entry = jnp.broadcast_to(table_row(c, r), (8, LANES))
            found = jnp.take_along_axis(entry, lane_idx, axis=1, mode="promise_in_bounds")
            acc[c] = jnp.where(hit, found, acc[c])
    return acc


def scatter_terms(height, row_idx, lane_idx, values):
    n = row_idx.shape[1]
    row_hit = row_idx == lax.broadcasted_iota(jnp.int32, (height, n), 0)
    lane_hit = lane_idx == lax.broadcasted_iota(jnp.int32, (LANES, n), 0)
    parts = []
    for v in values:
        upper = v.astype(BF16).astype(F32)
        for part in (upper, v - upper):
            parts.append(jnp.where(row_hit, jnp.broadcast_to(part, (height, n)), 0.0))
    left = jnp.concatenate(parts, axis=0).astype(BF16)
    right = jnp.where(lane_hit, 1.0, 0.0).astype(BF16)
    return lax.dot_general(left, right, (((1,), (1,)), ((), ())), preferred_element_type=F32)


def widen(table, slot_rows):
    return jnp.concatenate([table(g)[:, slot_rows] for g in range(GROUPS)], axis=1)


def split_rows(ref, store):
    for q in range(ROWS):
        for c in range(3):
            store(c, q, ref[c : c + 1, q * LANES : (q + 1) * LANES])


def substeps(pos, vel, total, shifted, attached, inv_mass, stiff, tie):
    for _ in range(SUBSTEPS):
        for c in range(len(pos)):
            before, after = shifted(pos[c])
            laplace = after - 2.0 * pos[c] + before
            accel = inv_mass * (stiff * laplace + tie * (attached[c] - pos[c]))
            vel[c] = vel[c] + DT_FINE * accel
            pos[c] = pos[c] + DT_FINE * vel[c]
            total[c] = total[c] + pos[c]


def exchange_kernel(
    disp,
    hex_nodes,
    modulus,
    yielded,
    stiffness,
    send_slots,
    fine_slot,
    fine_disp,
    fine_velo,
    fine_inv_mass,
    fine_stiff,
    tie_stiff,
    returned,
    internal,
    pos_out,
    vel_out,
    ext,
    corner,
    force,
    force_in,
    picked,
    received,
    table,
    outgoing,
    edge_out,
    edge_in,
    tied_out,
    tied_in,
    a2a_send,
    a2a_recv,
    halo_send,
    halo_recv,
):
    me, sub = lax.axis_index("mesh"), lax.axis_index("sub")
    n_sub = lax.axis_size("sub")
    top = sub == n_sub - 1
    low = sub == 0
    after = (jnp.where(top, lax.rem(me + 1, PEERS), me), jnp.where(top, 0, sub + 1))
    before = (jnp.where(low, lax.rem(me + PEERS - 1, PEERS), me), jnp.where(low, n_sub - 1, sub - 1))

    barrier = pltpu.get_barrier_semaphore()

    def greet(k, carry):
        pl.semaphore_signal(barrier, inc=1, device_id=(lax.rem(me + k, PEERS), sub), device_id_type=MESH)
        return carry

    for neighbour in (before, after):
        pl.semaphore_signal(barrier, inc=1, device_id=neighbour, device_id_type=MESH)
    lax.fori_loop(1, PEERS, greet, 0)

    def to(neighbour, src, dst, which):
        return pltpu.make_async_remote_copy(
            src, dst, halo_send.at[which], halo_recv.at[which], device_id=neighbour, device_id_type=MESH
        )

    def put_disp(c, q, row):
        ext[c, RIM + q : RIM + q + 1, :] = row

    split_rows(disp, put_disp)

    slot_at = widen(lambda g: send_slots[g * CAP : (g + 1) * CAP, :], slice(0, CAP))
    found = []
    for b in range(ROWS // 8):
        at = slot_at[b * 8 : (b + 1) * 8]
        zero = jnp.zeros((8, LANES), F32)
        found.append(
            lane_lookup(
                [zero] * 3, lambda c, r: ext[c, RIM + r : RIM + r + 1, :], range(ROWS), at >> 7, at & (LANES - 1)
            )
        )
    pad = jnp.zeros((ROWS, LANES - 3 * CAP), F32)
    for g in range(GROUPS):
        cut = [jnp.concatenate([f[c] for f in found], axis=0)[:, g * CAP : (g + 1) * CAP] for c in range(3)]
        picked[g * ROWS : (g + 1) * ROWS] = jnp.concatenate(cut + [pad], axis=1).reshape(ROWS, 1, LANES)

    def put_pos(c, q, row):
        pos_out[c, q : q + 1, :] = row

    def put_vel(c, q, row):
        vel_out[c, q : q + 1, :] = row

    split_rows(fine_disp, put_pos)
    split_rows(fine_velo, put_vel)
    for side, q in ((0, 0), (1, ROWS - 1)):
        for c in range(3):
            edge_out[side, c : c + 1, :] = pos_out[c, q : q + 1, :]
            edge_out[side, 3 + c : 4 + c, :] = vel_out[c, q : q + 1, :]
        edge_out[side, 6:7, :] = fine_inv_mass[q : q + 1, :]
        edge_out[side, 7:8, :] = fine_stiff[q : q + 1, :]
        edge_out[side, 8:9, :] = tie_stiff[q : q + 1, :]
        edge_out[side, 9:16, :] = jnp.zeros((7, LANES), F32)

    def own_corner(t, carry):
        cols = pl.ds(pl.multiple_of(t * LANES, LANES), LANES)
        at = hex_nodes[:, cols] + RIM * LANES
        zero = jnp.zeros((8, LANES), F32)
        got = lane_lookup(
            [zero] * 3, lambda c, r: ext[c, r : r + 1, :], range(RIM, RIM + ROWS), at >> 7, at & (LANES - 1)
        )
        for c in range(3):
            corner[c * 8 : (c + 1) * 8, cols] = got[c]
        return carry

    lax.fori_loop(0, ELEMS // LANES, own_corner, 0)

    pl.semaphore_wait(barrier, PEERS + 1)

    halos = [
        to(after, ext.at[:, pl.ds(ROWS, RIM), :], ext.at[:, pl.ds(0, RIM), :], 0),
        to(before, ext.at[:, pl.ds(RIM, RIM), :], ext.at[:, pl.ds(RIM + ROWS, RIM), :], 1),
        to(before, edge_out.at[0], edge_in.at[1], 2),
        to(after, edge_out.at[1], edge_in.at[0], 3),
    ]
    for copy in halos[:2]:
        copy.start()

    def all_to_all(src, dst, which):
        def send(k, carry):
            peer = lax.rem(me + k, PEERS)
            pltpu.make_async_remote_copy(
                src.at[peer],
                dst.at[me],
                a2a_send.at[which],
                a2a_recv.at[which],
                device_id=(peer, sub),
                device_id_type=MESH,
            ).start()
            return carry

        lax.fori_loop(1, PEERS, send, 0)
        dst[pl.ds(me, 1)] = src[pl.ds(me, 1)]
        return pltpu.make_async_remote_copy(
            src.at[pl.ds(0, PEERS - 1)],
            dst.at[pl.ds(0, PEERS - 1)],
            a2a_send.at[which],
            a2a_recv.at[which],
            device_id=after,
            device_id_type=MESH,
        )

    first = all_to_all(picked, received, 0)
    for copy in halos[2:]:
        copy.start()

    force[...] = jnp.zeros_like(force)
    for copy in halos[:2]:
        copy.wait()

    def rim_corner(t, carry):
        cols = pl.ds(pl.multiple_of(t * LANES, LANES), LANES)
        at = hex_nodes[:, cols] + RIM * LANES
        got = lane_lookup(
            [corner[c * 8 : (c + 1) * 8, cols] for c in range(3)],
            lambda c, r: ext[c, r : r + 1, :],
            [*range(RIM), *range(RIM + ROWS, EXT)],
            at >> 7,
            at & (LANES - 1),
        )
        for c in range(3):
            corner[c * 8 : (c + 1) * 8, cols] = got[c]
        return carry

    lax.fori_loop(0, ELEMS // LANES, rim_corner, 0)

    def element_force(t, carry):
        cols = pl.ds(pl.multiple_of(t * CHUNK, CHUNK), CHUNK)
        factor = modulus[:, cols] * jnp.where(yielded[:, cols] == 1, PLASTIC, 1.0)
        element = (
            jnp.dot(stiffness[...], corner[:, cols], precision=lax.Precision.HIGHEST, preferred_element_type=F32)
            * factor
        )
        at = hex_nodes[:, cols] + RIM * LANES
        row_at, lane_at = at >> 7, at & (LANES - 1)
        for k in range(8):
            force[...] += scatter_terms(
                EXT, row_at[k : k + 1], lane_at[k : k + 1], [element[c * 8 + k : c * 8 + k + 1] for c in range(3)]
            )
        return carry

    lax.fori_loop(0, ELEMS // CHUNK, element_force, 0)
    for c in range(3):
        ext_force = force[2 * c * EXT : (2 * c + 1) * EXT, :] + force[(2 * c + 1) * EXT : (2 * c + 2) * EXT, :]
        force[2 * c * EXT : (2 * c + 1) * EXT, :] = ext_force
        force_in[2, c] = ext_force[:RIM]
        force_in[3, c] = ext_force[RIM + ROWS :]
    rims = [
        to(before, force_in.at[2], force_in.at[1], 4),
        to(after, force_in.at[3], force_in.at[0], 5),
    ]
    for copy in rims:
        copy.start()

    first.wait_recv()
    for c in range(3):
        table[c] = widen(lambda g: received[g * ROWS : (g + 1) * ROWS].reshape(ROWS, LANES), slice(c * CAP, (c + 1) * CAP))
    slot = fine_slot[...]
    row_at = (slot >> 5) & (ROWS - 1)
    lane_at = ((slot >> 10) << 5) | (slot & (CAP - 1))
    blocks = []
    for b in range(ROWS // 8):
        zero = jnp.zeros((8, LANES), F32)
        blocks.append(
            lane_lookup(
                [zero] * 3,
                lambda c, r: table[c, r : r + 1, :],
                range(ROWS),
                row_at[b * 8 : (b + 1) * 8],
                lane_at[b * 8 : (b + 1) * 8],
            )
        )
    attached = [jnp.concatenate([b[c] for b in blocks], axis=0) for c in range(3)]
    none = jnp.zeros((5, LANES), F32)
    tied_out[0] = jnp.concatenate([a[:1] for a in attached] + [none], axis=0)
    tied_out[1] = jnp.concatenate([a[ROWS - 1 :] for a in attached] + [none], axis=0)
    ties = [to(before, tied_out.at[0], tied_in.at[1], 6), to(after, tied_out.at[1], tied_in.at[0], 7)]
    for copy in ties:
        copy.start()

    lane = lax.broadcasted_iota(jnp.int32, (ROWS, LANES), 1)

    def shifted(x):
        right = pltpu.roll(x, 1, 1)
        left = pltpu.roll(x, LANES - 1, 1)
        prev = jnp.where(lane == 0, pltpu.roll(right, 1, 0), right)
        nxt = jnp.where(lane == LANES - 1, pltpu.roll(left, ROWS - 1, 0), left)
        return prev, nxt

    pos = [pos_out[c] for c in range(3)]
    vel = [vel_out[c] for c in range(3)]
    total = [jnp.zeros((ROWS, LANES), F32) for _ in range(3)]
    im, st, tie = fine_inv_mass[...], fine_stiff[...], tie_stiff[...]
    first_rows = [x[:1] for x in pos + vel + [im, st, tie] + attached]
    last_rows = [x[ROWS - 1 :] for x in pos + vel + [im, st, tie] + attached]
    substeps(pos, vel, total, shifted, attached, im, st, tie)

    for copy in halos[2:] + ties:
        copy.wait()
    strip_lane = lax.broadcasted_iota(jnp.int32, (1, LANES), 1)
    starts = (me == 0) & (sub == 0)
    ends = (me == PEERS - 1) & (sub == n_sub - 1)

    def head(row, ghost):
        ghost = jnp.where(starts, 0.0, pltpu.roll(ghost, EDGE, 1))
        return jnp.where(strip_lane < EDGE, ghost, pltpu.roll(row, EDGE, 1))

    def tail(row, ghost):
        ghost = jnp.where(ends, 0.0, pltpu.roll(ghost, LANES - EDGE, 1))
        return jnp.where(strip_lane >= LANES - EDGE, ghost, pltpu.roll(row, LANES - EDGE, 1))

    ghost_head = [edge_in[0, i : i + 1, :] for i in range(9)] + [tied_in[0, c : c + 1, :] for c in range(3)]
    ghost_tail = [edge_in[1, i : i + 1, :] for i in range(9)] + [tied_in[1, c : c + 1, :] for c in range(3)]
    heads = [head(r, g) for r, g in zip(first_rows, ghost_head)]
    tails = [tail(r, g) for r, g in zip(last_rows, ghost_tail)]
    blank = jnp.zeros((2, LANES), F32)

    def strip(picks):
        return jnp.concatenate([heads[i] for i in picks] + [tails[i] for i in picks] + [blank], axis=0)

    strip_pos, strip_vel, strip_total = [strip((0, 1, 2))], [strip((3, 4, 5))], [jnp.zeros((8, LANES), F32)]
    substeps(
        strip_pos,
        strip_vel,
        strip_total,
        lambda x: (pltpu.roll(x, 1, 1), pltpu.roll(x, LANES - 1, 1)),
        [strip((9, 10, 11))],
        strip((6, 6, 6)),
        strip((7, 7, 7)),
        strip((8, 8, 8)),
    )
    sub_row = lax.broadcasted_iota(jnp.int32, (ROWS, LANES), 0)
    at_head = (sub_row == 0) & (lane < EDGE)
    at_tail = (sub_row == ROWS - 1) & (lane >= LANES - EDGE)

    def put_ends(whole, strips):
        forward = pltpu.roll(strips, LANES - EDGE, 1)
        back = pltpu.roll(strips, EDGE, 1)
        out = []
        for c in range(3):
            x = jnp.where(at_head, jnp.broadcast_to(forward[c : c + 1], (ROWS, LANES)), whole[c])
            out.append(jnp.where(at_tail, jnp.broadcast_to(back[3 + c : 4 + c], (ROWS, LANES)), x))
        return out

    pos = put_ends(pos, strip_pos[0])
    vel = put_ends(vel, strip_vel[0])
    total = put_ends(total, strip_total[0])
    for c in range(3):
        pos_out[c] = pos[c]
        vel_out[c] = vel[c]

    sums = None
    pull = [tie * (total[c] * (1.0 / SUBSTEPS) - attached[c]) for c in range(3)]
    for q in range(0, ROWS, 4):

        def flat(x):
            return jnp.concatenate([x[q + i : q + i + 1] for i in range(4)], axis=1)

        term = scatter_terms(ROWS, flat(row_at), flat(lane_at), [flat(p) for p in pull])
        sums = term if sums is None else sums + term
    force_at = [sums[2 * c * ROWS : (2 * c + 1) * ROWS] + sums[(2 * c + 1) * ROWS : (2 * c + 2) * ROWS] for c in range(3)]
    for g in range(GROUPS):
        cut = [f[:, g * CAP : (g + 1) * CAP] for f in force_at]
        outgoing[g * ROWS : (g + 1) * ROWS] = jnp.concatenate(cut + [pad], axis=1).reshape(ROWS, 1, LANES)
    second = all_to_all(outgoing, returned, 1)

    for copy in rims:
        copy.wait()
    for c in range(3):
        own = force[2 * c * EXT + RIM : 2 * c * EXT + RIM + ROWS, :]
        internal[c, :RIM] = own[:RIM] + force_in[0, c]
        internal[c, RIM : ROWS - RIM] = own[RIM : ROWS - RIM]
        internal[c, ROWS - RIM :] = own[ROWS - RIM :] + force_in[1, c]
    first.wait_send()
    second.wait()


def update_kernel(
    disp, velo, inv_mass, send_slots, returned, internal, pos, vel, disp_new, velo_new, pos_out, vel_out
):
    slot_at = widen(lambda g: send_slots[g * CAP : (g + 1) * CAP, :], slice(0, CAP))
    back = [
        widen(lambda g: returned[g * ROWS : (g + 1) * ROWS].reshape(ROWS, LANES), slice(c * CAP, (c + 1) * CAP))
        for c in range(3)
    ]
    row_at, lane_at = slot_at >> 7, slot_at & (LANES - 1)
    sums = None
    for q in range(0, ROWS, 4):

        def flat(x):
            return jnp.concatenate([x[q + i : q + i + 1] for i in range(4)], axis=1)

        term = scatter_terms(ROWS, flat(row_at), flat(lane_at), [flat(b) for b in back])
        sums = term if sums is None else sums + term
    change = []
    for c in range(3):
        coupling = sums[2 * c * ROWS : (2 * c + 1) * ROWS] + sums[(2 * c + 1) * ROWS : (2 * c + 2) * ROWS]
        change.append(inv_mass[...] * (coupling - internal[c]))
    for q in range(ROWS):
        cols = slice(q * LANES, (q + 1) * LANES)

        def three(x):
            return jnp.concatenate([x(c) for c in range(3)], axis=0)

        v = velo[:, cols] + DT_COARSE * three(lambda c: change[c][q : q + 1])
        velo_new[:, cols] = v
        disp_new[:, cols] = disp[:, cols] + DT_COARSE * v
        pos_out[:, cols] = three(lambda c: pos[c, q : q + 1, :])
        vel_out[:, cols] = three(lambda c: vel[c, q : q + 1, :])


def on_device(
    disp,
    velo,
    inv_mass,
    hex_nodes,
    modulus,
    yielded,
    stiffness,
    send_slots,
    fine_slot,
    fine_disp,
    fine_velo,
    fine_inv_mass,
    fine_stiff,
    tie_stiff,
):
    vmem = pl.BlockSpec(memory_space=pltpu.VMEM)
    chain = jax.ShapeDtypeStruct((3, ROWS, LANES), F32)
    flat = jax.ShapeDtypeStruct(disp.shape, F32)
    rows = lambda x: x.reshape(ROWS, LANES)
    line = lambda x: x.reshape(1, ELEMS)
    buffer = lambda *shape: pltpu.VMEM(shape, F32)
    returned, internal, pos, vel = pl.pallas_call(
        exchange_kernel,
        out_shape=(jax.ShapeDtypeStruct((PEERS, 1, LANES), F32), chain, chain, chain),
        in_specs=[vmem] * 12,
        out_specs=(vmem,) * 4,
        scratch_shapes=[
            buffer(3, EXT, LANES),
            buffer(24, ELEMS),
            buffer(6 * EXT, LANES),
            buffer(4, 3, RIM, LANES),
            buffer(PEERS, 1, LANES),
            buffer(PEERS, 1, LANES),
            buffer(3, ROWS, LANES),
            buffer(PEERS, 1, LANES),
            buffer(2, 16, LANES),
            buffer(2, 16, LANES),
            buffer(2, 8, LANES),
            buffer(2, 8, LANES),
            pltpu.SemaphoreType.DMA((2,)),
            pltpu.SemaphoreType.DMA((2,)),
            pltpu.SemaphoreType.DMA((8,)),
            pltpu.SemaphoreType.DMA((8,)),
        ],
        compiler_params=pltpu.CompilerParams(
            collective_id=0, has_side_effects=True, vmem_limit_bytes=32 * 1024 * 1024
        ),
        name="exchange",
    )(
        disp,
        hex_nodes,
        line(modulus),
        line(yielded),
        stiffness,
        send_slots,
        rows(fine_slot),
        fine_disp,
        fine_velo,
        rows(fine_inv_mass),
        rows(fine_stiff),
        rows(tie_stiff),
    )
    return pl.pallas_call(
        update_kernel,
        out_shape=(flat,) * 4,
        in_specs=[vmem] * 8,
        out_specs=(vmem,) * 4,
        compiler_params=pltpu.CompilerParams(vmem_limit_bytes=32 * 1024 * 1024),
        name="update",
    )(disp, velo, rows(inv_mass), send_slots, returned, internal, pos, vel)


def solution(mesh):
    placed = (
        P(None, ("mesh", "sub")),
        P(None, ("mesh", "sub")),
        P(("mesh", "sub")),
        P(None, ("mesh", "sub")),
        P(("mesh", "sub")),
        P(("mesh", "sub")),
        P(),
        P(("mesh", "sub"), None),
        P(("mesh", "sub")),
        P(None, ("mesh", "sub")),
        P(None, ("mesh", "sub")),
        P(("mesh", "sub")),
        P(("mesh", "sub")),
        P(("mesh", "sub")),
    )
    return jax.shard_map(
        on_device,
        mesh=mesh,
        in_specs=placed,
        out_specs=(
            P(None, ("mesh", "sub")),
            P(None, ("mesh", "sub")),
            P(None, ("mesh", "sub")),
            P(None, ("mesh", "sub")),
        ),
        check_vma=False,
    )
```

```python
import jax
import jax.numpy as jnp
from jax import lax
from jax.experimental import pallas as pl
from jax.experimental.pallas import tpu as pltpu
from jax.sharding import PartitionSpec as P

SUBSTEPS = 8
DT_FINE = 0.5
DT_COARSE = 1.0
PLASTIC = 0.3

LANES = 128
CAP = 32
PEERS = 128
RING = 8
ROWS = 32
RIM = 8
EXT = ROWS + 2 * RIM
ELEMS = 2048
CHUNK = 512
EDGE = 8
MESH = pl.DeviceIdType.MESH
F32 = jnp.float32
BF16 = jnp.bfloat16


def lane_lookup(acc, table_row, rows, row_idx, lane_idx):
    acc = list(acc)
    for r in rows:
        hit = row_idx == r
        for c in range(3):
            entry = jnp.broadcast_to(table_row(c, r), (8, LANES))
            found = jnp.take_along_axis(entry, lane_idx, axis=1, mode="promise_in_bounds")
            acc[c] = jnp.where(hit, found, acc[c])
    return acc


def scatter_terms(height, row_idx, lane_idx, values):
    n = row_idx.shape[1]
    row_hit = row_idx == lax.broadcasted_iota(jnp.int32, (height, n), 0)
    lane_hit = lane_idx == lax.broadcasted_iota(jnp.int32, (LANES, n), 0)
    parts = []
    for v in values:
        upper = v.astype(BF16).astype(F32)
        for part in (upper, v - upper):
            parts.append(jnp.where(row_hit, jnp.broadcast_to(part, (height, n)), 0.0))
    left = jnp.concatenate(parts, axis=0).astype(BF16)
    right = jnp.where(lane_hit, 1.0, 0.0).astype(BF16)
    return lax.dot_general(left, right, (((1,), (1,)), ((), ())), preferred_element_type=F32)


def flat(x, q):
    return jnp.concatenate([x[q + i : q + i + 1] for i in range(4)], axis=1)


def joined(sums, height):
    return [
        sums[2 * c * height : (2 * c + 1) * height] + sums[(2 * c + 1) * height : (2 * c + 2) * height] for c in range(3)
    ]


def by_slot(parts):
    stacked = jnp.concatenate([*parts, jnp.zeros((LANES - 3 * CAP, PEERS), F32)], axis=0)
    return jnp.transpose(stacked).reshape(PEERS, 1, LANES)


def split_rows(ref, store):
    for q in range(ROWS):
        for c in range(3):
            store(c, q, ref[c : c + 1, q * LANES : (q + 1) * LANES])


def substeps(pos, vel, total, shifted, attached, inv_mass, stiff, tie):
    for _ in range(SUBSTEPS):
        for c in range(len(pos)):
            before, after = shifted(pos[c])
            laplace = after - 2.0 * pos[c] + before
            accel = inv_mass * (stiff * laplace + tie * (attached[c] - pos[c]))
            vel[c] = vel[c] + DT_FINE * accel
            pos[c] = pos[c] + DT_FINE * vel[c]
            total[c] = total[c] + pos[c]


def exchange_kernel(
    disp_arg,
    send_slots_arg,
    fine_disp_arg,
    fine_velo_arg,
    fine_inv_mass_arg,
    fine_stiff_arg,
    tie_stiff_arg,
    hex_nodes_arg,
    fine_slot_arg,
    modulus_arg,
    yielded_arg,
    stiffness_arg,
    returned,
    internal,
    pos_out,
    vel_out,
    disp,
    send_slots,
    fine_disp,
    fine_velo,
    fine_inv_mass,
    fine_stiff,
    tie_stiff,
    hex_nodes,
    fine_slot,
    modulus,
    yielded,
    stiffness,
    ext,
    corner,
    force,
    force_in,
    picked,
    received,
    table,
    outgoing,
    edge_out,
    edge_in,
    tied_out,
    tied_in,
    a2a_send,
    a2a_recv,
    halo_send,
    halo_recv,
    load_sem,
):
    loads = [
        pltpu.make_async_copy(src, dst, load_sem.at[i])
        for i, (src, dst) in enumerate(
            (
                (disp_arg, disp),
                (send_slots_arg, send_slots),
                (fine_disp_arg, fine_disp),
                (fine_velo_arg, fine_velo),
                (fine_inv_mass_arg, fine_inv_mass),
                (fine_stiff_arg, fine_stiff),
                (tie_stiff_arg, tie_stiff),
                (hex_nodes_arg, hex_nodes),
                (fine_slot_arg, fine_slot),
                (modulus_arg, modulus),
                (yielded_arg, yielded),
                (stiffness_arg, stiffness),
            )
        )
    ]
    for load in loads:
        load.start()
    me, sub = lax.axis_index("mesh"), lax.axis_index("sub")
    n_sub = lax.axis_size("sub")
    top = sub == n_sub - 1
    low = sub == 0
    after = (jnp.where(top, lax.rem(me + 1, PEERS), me), jnp.where(top, 0, sub + 1))
    before = (jnp.where(low, lax.rem(me + PEERS - 1, PEERS), me), jnp.where(low, n_sub - 1, sub - 1))

    barrier = pltpu.get_barrier_semaphore()

    y, z, core = me // (2 * RING), lax.rem(me // 2, RING), lax.rem(me, 2)
    y_at = [lax.rem(y + i, RING) * (2 * RING) for i in range(RING)]
    z_at = [lax.rem(z + i, RING) * 2 for i in range(RING)]
    core_at = [core, 1 - core]
    hops = lambda i: min(i, RING - i)
    steps = [(dy, dz, dc) for dy in range(RING) for dz in range(RING) for dc in range(2) if (dy, dz, dc) != (0, 0, 0)]
    steps.sort(key=lambda step: -(2 * (hops(step[0]) + hops(step[1])) + step[2]))
    peers = [y_at[dy] + z_at[dz] + core_at[dc] for dy, dz, dc in steps]

    for neighbour in (before, after):
        pl.semaphore_signal(barrier, inc=1, device_id=neighbour, device_id_type=MESH)
    for peer in peers:
        pl.semaphore_signal(barrier, inc=1, device_id=(peer, sub), device_id_type=MESH)

    def to(neighbour, src, dst, which):
        return pltpu.make_async_remote_copy(
            src, dst, halo_send.at[which], halo_recv.at[which], device_id=neighbour, device_id_type=MESH
        )

    def put_disp(c, q, row):
        ext[c, RIM + q : RIM + q + 1, :] = row

    for load in loads[:2]:
        load.wait()
    split_rows(disp, put_disp)

    zero = jnp.zeros((8, LANES), F32)
    found = []
    for b in range(CAP // 8):
        at = send_slots[b * 8 : (b + 1) * 8]
        found.append(
            lane_lookup(
                [zero] * 3, lambda c, r: ext[c, RIM + r : RIM + r + 1, :], range(ROWS), at >> 7, at & (LANES - 1)
            )
        )
    picked[...] = by_slot([jnp.concatenate([f[c] for f in found], axis=0) for c in range(3)])

    def put_pos(c, q, row):
        pos_out[c, q : q + 1, :] = row

    def put_vel(c, q, row):
        vel_out[c, q : q + 1, :] = row

    for load in loads[2:7]:
        load.wait()
    split_rows(fine_disp, put_pos)
    split_rows(fine_velo, put_vel)
    for side, q in ((0, 0), (1, ROWS - 1)):
        for c in range(3):
            edge_out[side, c : c + 1, :] = pos_out[c, q : q + 1, :]
            edge_out[side, 3 + c : 4 + c, :] = vel_out[c, q : q + 1, :]
        edge_out[side, 6:7, :] = fine_inv_mass[q : q + 1, :]
        edge_out[side, 7:8, :] = fine_stiff[q : q + 1, :]
        edge_out[side, 8:9, :] = tie_stiff[q : q + 1, :]
        edge_out[side, 9:16, :] = jnp.zeros((7, LANES), F32)

    for load in loads[7:]:
        load.wait()

    def own_corner(t, carry):
        cols = pl.ds(pl.multiple_of(t * LANES, LANES), LANES)
        at = hex_nodes[:, cols] + RIM * LANES
        zero = jnp.zeros((8, LANES), F32)
        got = lane_lookup(
            [zero] * 3, lambda c, r: ext[c, r : r + 1, :], range(RIM, RIM + ROWS), at >> 7, at & (LANES - 1)
        )
        for c in range(3):
            corner[c * 8 : (c + 1) * 8, cols] = got[c]
        return carry

    lax.fori_loop(0, ELEMS // LANES, own_corner, 0)

    pl.semaphore_wait(barrier, PEERS + 1)

    halos = [
        to(after, ext.at[:, pl.ds(ROWS, RIM), :], ext.at[:, pl.ds(0, RIM), :], 0),
        to(before, ext.at[:, pl.ds(RIM, RIM), :], ext.at[:, pl.ds(RIM + ROWS, RIM), :], 1),
        to(before, edge_out.at[0], edge_in.at[1], 2),
        to(after, edge_out.at[1], edge_in.at[0], 3),
    ]
    for copy in halos[:2]:
        copy.start()

    def all_to_all(src, dst, which):
        for peer in peers:
            pltpu.make_async_remote_copy(
                src.at[peer],
                dst.at[me],
                a2a_send.at[which],
                a2a_recv.at[which],
                device_id=(peer, sub),
                device_id_type=MESH,
            ).start()
        dst[pl.ds(me, 1)] = src[pl.ds(me, 1)]
        return pltpu.make_async_remote_copy(
            src.at[pl.ds(0, PEERS - 1)],
            dst.at[pl.ds(0, PEERS - 1)],
            a2a_send.at[which],
            a2a_recv.at[which],
            device_id=after,
            device_id_type=MESH,
        )

    first = all_to_all(picked, received, 0)
    for copy in halos[2:]:
        copy.start()

    force[...] = jnp.zeros_like(force)
    for copy in halos[:2]:
        copy.wait()

    def rim_corner(t, carry):
        cols = pl.ds(pl.multiple_of(t * LANES, LANES), LANES)
        at = hex_nodes[:, cols] + RIM * LANES
        got = lane_lookup(
            [corner[c * 8 : (c + 1) * 8, cols] for c in range(3)],
            lambda c, r: ext[c, r : r + 1, :],
            [*range(RIM), *range(RIM + ROWS, EXT)],
            at >> 7,
            at & (LANES - 1),
        )
        for c in range(3):
            corner[c * 8 : (c + 1) * 8, cols] = got[c]
        return carry

    lax.fori_loop(0, ELEMS // LANES, rim_corner, 0)

    def element_force(t, carry):
        cols = pl.ds(pl.multiple_of(t * CHUNK, CHUNK), CHUNK)
        factor = modulus[:, cols] * jnp.where(yielded[:, cols] == 1, PLASTIC, 1.0)
        element = (
            jnp.dot(stiffness[...], corner[:, cols], precision=lax.Precision.HIGHEST, preferred_element_type=F32)
            * factor
        )
        at = hex_nodes[:, cols] + RIM * LANES
        row_at, lane_at = at >> 7, at & (LANES - 1)
        for k in range(8):
            force[...] += scatter_terms(
                EXT, row_at[k : k + 1], lane_at[k : k + 1], [element[c * 8 + k : c * 8 + k + 1] for c in range(3)]
            )
        return carry

    first.wait_recv()
    table[...] = jnp.transpose(received[...].reshape(PEERS, LANES))
    slot = fine_slot[...]
    row_at, lane_at = slot & (CAP - 1), slot >> 5
    blocks = []
    for b in range(ROWS // 8):
        zero = jnp.zeros((8, LANES), F32)
        blocks.append(
            lane_lookup(
                [zero] * 3,
                lambda c, r: table[c * CAP + r : c * CAP + r + 1, :],
                range(CAP),
                row_at[b * 8 : (b + 1) * 8],
                lane_at[b * 8 : (b + 1) * 8],
            )
        )
    attached = [jnp.concatenate([b[c] for b in blocks], axis=0) for c in range(3)]
    none = jnp.zeros((5, LANES), F32)
    tied_out[0] = jnp.concatenate([a[:1] for a in attached] + [none], axis=0)
    tied_out[1] = jnp.concatenate([a[ROWS - 1 :] for a in attached] + [none], axis=0)
    ties = [to(before, tied_out.at[0], tied_in.at[1], 6), to(after, tied_out.at[1], tied_in.at[0], 7)]
    for copy in ties:
        copy.start()

    lane = lax.broadcasted_iota(jnp.int32, (ROWS, LANES), 1)

    def shifted(x):
        right = pltpu.roll(x, 1, 1)
        left = pltpu.roll(x, LANES - 1, 1)
        prev = jnp.where(lane == 0, pltpu.roll(right, 1, 0), right)
        nxt = jnp.where(lane == LANES - 1, pltpu.roll(left, ROWS - 1, 0), left)
        return prev, nxt

    pos = [pos_out[c] for c in range(3)]
    vel = [vel_out[c] for c in range(3)]
    total = [jnp.zeros((ROWS, LANES), F32) for _ in range(3)]
    im, st, tie = fine_inv_mass[...], fine_stiff[...], tie_stiff[...]
    first_rows = [x[:1] for x in pos + vel + [im, st, tie] + attached]
    last_rows = [x[ROWS - 1 :] for x in pos + vel + [im, st, tie] + attached]
    substeps(pos, vel, total, shifted, attached, im, st, tie)

    sub_row = lax.broadcasted_iota(jnp.int32, (ROWS, LANES), 0)
    at_head = (sub_row == 0) & (lane < EDGE)
    at_tail = (sub_row == ROWS - 1) & (lane >= LANES - EDGE)
    at_ends = at_head | at_tail

    def tie_force(sum_of_pos):
        return [tie * (sum_of_pos[c] * (1.0 / SUBSTEPS) - attached[c]) for c in range(3)]

    pull = [jnp.where(at_ends, 0.0, p) for p in tie_force(total)]
    sums = None
    for q in range(0, ROWS, 4):
        term = scatter_terms(CAP, flat(row_at, q), flat(lane_at, q), [flat(p, q) for p in pull])
        sums = term if sums is None else sums + term

    lax.fori_loop(0, 2, element_force, 0)
    for copy in halos[2:] + ties:
        copy.wait()
    strip_lane = lax.broadcasted_iota(jnp.int32, (1, LANES), 1)
    starts = (me == 0) & (sub == 0)
    ends = (me == PEERS - 1) & (sub == n_sub - 1)

    def head(row, ghost):
        ghost = jnp.where(starts, 0.0, pltpu.roll(ghost, EDGE, 1))
        return jnp.where(strip_lane < EDGE, ghost, pltpu.roll(row, EDGE, 1))

    def tail(row, ghost):
        ghost = jnp.where(ends, 0.0, pltpu.roll(ghost, LANES - EDGE, 1))
        return jnp.where(strip_lane >= LANES - EDGE, ghost, pltpu.roll(row, LANES - EDGE, 1))

    ghost_head = [edge_in[0, i : i + 1, :] for i in range(9)] + [tied_in[0, c : c + 1, :] for c in range(3)]
    ghost_tail = [edge_in[1, i : i + 1, :] for i in range(9)] + [tied_in[1, c : c + 1, :] for c in range(3)]
    heads = [head(r, g) for r, g in zip(first_rows, ghost_head)]
    tails = [tail(r, g) for r, g in zip(last_rows, ghost_tail)]
    blank = jnp.zeros((2, LANES), F32)

    def strip(picks):
        return jnp.concatenate([heads[i] for i in picks] + [tails[i] for i in picks] + [blank], axis=0)

    strip_pos, strip_vel, strip_total = [strip((0, 1, 2))], [strip((3, 4, 5))], [jnp.zeros((8, LANES), F32)]
    substeps(
        strip_pos,
        strip_vel,
        strip_total,
        lambda x: (pltpu.roll(x, 1, 1), pltpu.roll(x, LANES - 1, 1)),
        [strip((9, 10, 11))],
        strip((6, 6, 6)),
        strip((7, 7, 7)),
        strip((8, 8, 8)),
    )
    def put_ends(whole, strips):
        forward = pltpu.roll(strips, LANES - EDGE, 1)
        back = pltpu.roll(strips, EDGE, 1)
        out = []
        for c in range(3):
            x = jnp.where(at_head, jnp.broadcast_to(forward[c : c + 1], (ROWS, LANES)), whole[c])
            out.append(jnp.where(at_tail, jnp.broadcast_to(back[3 + c : 4 + c], (ROWS, LANES)), x))
        return out

    pos = put_ends(pos, strip_pos[0])
    vel = put_ends(vel, strip_vel[0])
    total = put_ends(total, strip_total[0])
    end_pull = [jnp.where(at_ends, p, 0.0) for p in tie_force(total)]
    ends_of = lambda x: jnp.concatenate([x[:1], x[ROWS - 1 :]], axis=1)
    sums = sums + scatter_terms(CAP, ends_of(row_at), ends_of(lane_at), [ends_of(p) for p in end_pull])
    outgoing[...] = by_slot(joined(sums, CAP))
    second = all_to_all(outgoing, returned, 1)
    lax.fori_loop(2, 4, element_force, 0)
    for c in range(3):
        ext_force = force[2 * c * EXT : (2 * c + 1) * EXT, :] + force[(2 * c + 1) * EXT : (2 * c + 2) * EXT, :]
        force[2 * c * EXT : (2 * c + 1) * EXT, :] = ext_force
        force_in[2, c] = ext_force[:RIM]
        force_in[3, c] = ext_force[RIM + ROWS :]
    rims = [
        to(before, force_in.at[2], force_in.at[1], 4),
        to(after, force_in.at[3], force_in.at[0], 5),
    ]
    for copy in rims:
        copy.start()


    for c in range(3):
        pos_out[c] = pos[c]
        vel_out[c] = vel[c]
    for copy in rims:
        copy.wait()
    for c in range(3):
        own = force[2 * c * EXT + RIM : 2 * c * EXT + RIM + ROWS, :]
        internal[c, :RIM] = own[:RIM] + force_in[0, c]
        internal[c, RIM : ROWS - RIM] = own[RIM : ROWS - RIM]
        internal[c, ROWS - RIM :] = own[ROWS - RIM :] + force_in[1, c]
    first.wait_send()
    second.wait()


def update_kernel(
    disp, velo, inv_mass, send_slots, returned, internal, pos, vel, disp_new, velo_new, pos_out, vel_out
):
    slot_at = send_slots[...]
    back = jnp.transpose(returned[...].reshape(PEERS, LANES))
    back = [back[c * CAP : (c + 1) * CAP] for c in range(3)]
    row_at, lane_at = slot_at >> 7, slot_at & (LANES - 1)
    sums = None
    for q in range(0, CAP, 4):
        term = scatter_terms(ROWS, flat(row_at, q), flat(lane_at, q), [flat(b, q) for b in back])
        sums = term if sums is None else sums + term
    change = [inv_mass[...] * (coupling - internal[c]) for c, coupling in enumerate(joined(sums, ROWS))]
    for q in range(ROWS):
        cols = slice(q * LANES, (q + 1) * LANES)

        def three(x):
            return jnp.concatenate([x(c) for c in range(3)], axis=0)

        v = velo[:, cols] + DT_COARSE * three(lambda c: change[c][q : q + 1])
        velo_new[:, cols] = v
        disp_new[:, cols] = disp[:, cols] + DT_COARSE * v
        pos_out[:, cols] = three(lambda c: pos[c, q : q + 1, :])
        vel_out[:, cols] = three(lambda c: vel[c, q : q + 1, :])


def on_device(
    disp,
    velo,
    inv_mass,
    hex_nodes,
    modulus,
    yielded,
    stiffness,
    send_slots,
    fine_slot,
    fine_disp,
    fine_velo,
    fine_inv_mass,
    fine_stiff,
    tie_stiff,
):
    vmem = pl.BlockSpec(memory_space=pltpu.VMEM)
    chain = jax.ShapeDtypeStruct((3, ROWS, LANES), F32)
    flat = jax.ShapeDtypeStruct(disp.shape, F32)
    rows = lambda x: x.reshape(ROWS, LANES)
    line = lambda x: x.reshape(1, ELEMS)
    buffer = lambda *shape: pltpu.VMEM(shape, F32)
    slots = send_slots.T
    loaded = (
        disp,
        slots,
        fine_disp,
        fine_velo,
        rows(fine_inv_mass),
        rows(fine_stiff),
        rows(tie_stiff),
        hex_nodes,
        rows(fine_slot),
        line(modulus),
        line(yielded),
        stiffness,
    )
    returned, internal, pos, vel = pl.pallas_call(
        exchange_kernel,
        out_shape=(jax.ShapeDtypeStruct((PEERS, 1, LANES), F32), chain, chain, chain),
        in_specs=[pl.BlockSpec(memory_space=pltpu.HBM)] * 12,
        out_specs=(vmem,) * 4,
        scratch_shapes=[
            *[pltpu.VMEM(x.shape, x.dtype) for x in loaded],
            buffer(3, EXT, LANES),
            buffer(24, ELEMS),
            buffer(6 * EXT, LANES),
            buffer(4, 3, RIM, LANES),
            buffer(PEERS, 1, LANES),
            buffer(PEERS, 1, LANES),
            buffer(LANES, PEERS),
            buffer(PEERS, 1, LANES),
            buffer(2, 16, LANES),
            buffer(2, 16, LANES),
            buffer(2, 8, LANES),
            buffer(2, 8, LANES),
            pltpu.SemaphoreType.DMA((2,)),
            pltpu.SemaphoreType.DMA((2,)),
            pltpu.SemaphoreType.DMA((8,)),
            pltpu.SemaphoreType.DMA((8,)),
            pltpu.SemaphoreType.DMA((len(loaded),)),
        ],
        compiler_params=pltpu.CompilerParams(
            collective_id=0, has_side_effects=True, vmem_limit_bytes=32 * 1024 * 1024
        ),
        name="exchange",
    )(*[pltpu.with_memory_space_constraint(x, pltpu.HBM) for x in loaded])
    return pl.pallas_call(
        update_kernel,
        out_shape=(flat,) * 4,
        in_specs=[vmem] * 8,
        out_specs=(vmem,) * 4,
        compiler_params=pltpu.CompilerParams(vmem_limit_bytes=32 * 1024 * 1024),
        name="update",
    )(disp, velo, rows(inv_mass), slots, returned, internal, pos, vel)


def solution(mesh):
    placed = (
        P(None, ("mesh", "sub")),
        P(None, ("mesh", "sub")),
        P(("mesh", "sub")),
        P(None, ("mesh", "sub")),
        P(("mesh", "sub")),
        P(("mesh", "sub")),
        P(),
        P(("mesh", "sub"), None),
        P(("mesh", "sub")),
        P(None, ("mesh", "sub")),
        P(None, ("mesh", "sub")),
        P(("mesh", "sub")),
        P(("mesh", "sub")),
        P(("mesh", "sub")),
    )
    return jax.shard_map(
        on_device,
        mesh=mesh,
        in_specs=placed,
        out_specs=(
            P(None, ("mesh", "sub")),
            P(None, ("mesh", "sub")),
            P(None, ("mesh", "sub")),
            P(None, ("mesh", "sub")),
        ),
        check_vma=False,
    )
```

```python
import jax
import jax.numpy as jnp
from jax import lax
from jax.experimental import pallas as pl
from jax.experimental.pallas import tpu as pltpu
from jax.sharding import PartitionSpec as P

SUBSTEPS = 8
DT_FINE = 0.5
DT_COARSE = 1.0
PLASTIC = 0.3

LANES = 128
CAP = 32
PEERS = 128
RING = 8
ROWS = 32
RIM = 8
EXT = ROWS + 2 * RIM
ELEMS = 2048
CHUNK = 512
EDGE = 8
MESH = pl.DeviceIdType.MESH
F32 = jnp.float32
BF16 = jnp.bfloat16


def lane_lookup(acc, table_row, rows, row_idx, lane_idx):
    acc = list(acc)
    for r in rows:
        hit = row_idx == r
        for c in range(3):
            entry = jnp.broadcast_to(table_row(c, r), (8, LANES))
            found = jnp.take_along_axis(entry, lane_idx, axis=1, mode="promise_in_bounds")
            acc[c] = jnp.where(hit, found, acc[c])
    return acc


def scatter_terms(height, row_idx, lane_idx, values):
    n = row_idx.shape[1]
    row_hit = row_idx == lax.broadcasted_iota(jnp.int32, (height, n), 0)
    lane_hit = lane_idx == lax.broadcasted_iota(jnp.int32, (LANES, n), 0)
    parts = []
    for v in values:
        upper = v.astype(BF16).astype(F32)
        for part in (upper, v - upper):
            parts.append(jnp.where(row_hit, jnp.broadcast_to(part, (height, n)), 0.0))
    left = jnp.concatenate(parts, axis=0).astype(BF16)
    right = jnp.where(lane_hit, 1.0, 0.0).astype(BF16)
    return lax.dot_general(left, right, (((1,), (1,)), ((), ())), preferred_element_type=F32)


def flat(x, q):
    return jnp.concatenate([x[q + i : q + i + 1] for i in range(4)], axis=1)


def joined(sums, height):
    return [
        sums[2 * c * height : (2 * c + 1) * height] + sums[(2 * c + 1) * height : (2 * c + 2) * height] for c in range(3)
    ]


def by_slot(parts):
    stacked = jnp.concatenate([*parts, jnp.zeros((LANES - 3 * CAP, PEERS), F32)], axis=0)
    return jnp.transpose(stacked)


def split_rows(ref, store):
    for q in range(ROWS):
        for c in range(3):
            store(c, q, ref[c : c + 1, q * LANES : (q + 1) * LANES])


def substeps(pos, vel, total, shifted, attached, inv_mass, stiff, tie):
    for _ in range(SUBSTEPS):
        for c in range(len(pos)):
            before, after = shifted(pos[c])
            laplace = after - 2.0 * pos[c] + before
            accel = inv_mass * (stiff * laplace + tie * (attached[c] - pos[c]))
            vel[c] = vel[c] + DT_FINE * accel
            pos[c] = pos[c] + DT_FINE * vel[c]
            total[c] = total[c] + pos[c]


def exchange_kernel(
    disp_arg,
    send_slots_arg,
    fine_disp_arg,
    fine_velo_arg,
    fine_inv_mass_arg,
    fine_stiff_arg,
    tie_stiff_arg,
    hex_nodes_arg,
    fine_slot_arg,
    modulus_arg,
    yielded_arg,
    stiffness_arg,
    returned,
    internal,
    pos_flat,
    vel_flat,
    disp,
    send_slots,
    fine_disp,
    fine_velo,
    fine_inv_mass,
    fine_stiff,
    tie_stiff,
    hex_nodes,
    fine_slot,
    modulus,
    yielded,
    stiffness,
    pos_out,
    vel_out,
    ext,
    corner,
    force,
    force_in,
    picked,
    received,
    table,
    outgoing,
    edge_out,
    edge_in,
    tied_out,
    tied_in,
    a2a_send,
    a2a_recv,
    halo_send,
    halo_recv,
    load_sem,
):
    loads = [
        pltpu.make_async_copy(src, dst, load_sem.at[i])
        for i, (src, dst) in enumerate(
            (
                (disp_arg, disp),
                (send_slots_arg, send_slots),
                (fine_disp_arg, fine_disp),
                (fine_velo_arg, fine_velo),
                (fine_inv_mass_arg, fine_inv_mass),
                (fine_stiff_arg, fine_stiff),
                (tie_stiff_arg, tie_stiff),
                (hex_nodes_arg, hex_nodes),
                (fine_slot_arg, fine_slot),
                (modulus_arg, modulus),
                (yielded_arg, yielded),
                (stiffness_arg, stiffness),
            )
        )
    ]
    for load in loads:
        load.start()
    me, sub = lax.axis_index("mesh"), lax.axis_index("sub")
    n_sub = lax.axis_size("sub")
    top = sub == n_sub - 1
    low = sub == 0
    after = (jnp.where(top, lax.rem(me + 1, PEERS), me), jnp.where(top, 0, sub + 1))
    before = (jnp.where(low, lax.rem(me + PEERS - 1, PEERS), me), jnp.where(low, n_sub - 1, sub - 1))

    barrier = pltpu.get_barrier_semaphore()

    y, z, core = me // (2 * RING), lax.rem(me // 2, RING), lax.rem(me, 2)
    y_at = [lax.rem(y + i, RING) * (2 * RING) for i in range(RING)]
    z_at = [lax.rem(z + i, RING) * 2 for i in range(RING)]
    core_at = [core, 1 - core]
    hops = lambda i: min(i, RING - i)
    steps = [(dy, dz, dc) for dy in range(RING) for dz in range(RING) for dc in range(2) if (dy, dz, dc) != (0, 0, 0)]
    steps.sort(key=lambda step: -(2 * (hops(step[0]) + hops(step[1])) + step[2]))
    peers = [y_at[dy] + z_at[dz] + core_at[dc] for dy, dz, dc in steps]

    for peer in peers:
        pl.semaphore_signal(barrier, inc=1, device_id=(peer, sub), device_id_type=MESH)
    for neighbour in (before, after):
        pl.semaphore_signal(barrier, inc=1, device_id=neighbour, device_id_type=MESH)
    def to(neighbour, src, dst, which):
        return pltpu.make_async_remote_copy(
            src, dst, halo_send.at[which], halo_recv.at[which], device_id=neighbour, device_id_type=MESH
        )

    def put_disp(c, q, row):
        ext[c, RIM + q : RIM + q + 1, :] = row

    for load in loads[:2]:
        load.wait()
    split_rows(disp, put_disp)

    zero = jnp.zeros((8, LANES), F32)
    found = []
    for b in range(CAP // 8):
        at = send_slots[b * 8 : (b + 1) * 8]
        found.append(
            lane_lookup(
                [zero] * 3, lambda c, r: ext[c, RIM + r : RIM + r + 1, :], range(ROWS), at >> 7, at & (LANES - 1)
            )
        )
    picked[...] = by_slot([jnp.concatenate([f[c] for f in found], axis=0) for c in range(3)])

    def put_pos(c, q, row):
        pos_out[c, q : q + 1, :] = row

    def put_vel(c, q, row):
        vel_out[c, q : q + 1, :] = row

    for load in loads[2:7]:
        load.wait()
    split_rows(fine_disp, put_pos)
    split_rows(fine_velo, put_vel)
    for side, q in ((0, 0), (1, ROWS - 1)):
        for c in range(3):
            edge_out[side, c : c + 1, :] = pos_out[c, q : q + 1, :]
            edge_out[side, 3 + c : 4 + c, :] = vel_out[c, q : q + 1, :]
        edge_out[side, 6:7, :] = fine_inv_mass[q : q + 1, :]
        edge_out[side, 7:8, :] = fine_stiff[q : q + 1, :]
        edge_out[side, 8:9, :] = tie_stiff[q : q + 1, :]
        edge_out[side, 9:16, :] = jnp.zeros((7, LANES), F32)

    for load in loads[7:]:
        load.wait()

    pl.semaphore_wait(barrier, PEERS + 1)

    halos = [
        to(after, ext.at[:, pl.ds(ROWS, RIM), :], ext.at[:, pl.ds(0, RIM), :], 0),
        to(before, ext.at[:, pl.ds(RIM, RIM), :], ext.at[:, pl.ds(RIM + ROWS, RIM), :], 1),
        to(before, edge_out.at[0], edge_in.at[1], 2),
        to(after, edge_out.at[1], edge_in.at[0], 3),
    ]
    for copy in halos[:2]:
        copy.start()

    def all_to_all(src, dst, which):
        def send(peer):
            pltpu.make_async_remote_copy(
                src.at[pl.ds(peer, 1)],
                dst.at[pl.ds(me, 1)],
                a2a_send.at[which],
                a2a_recv.at[which],
                device_id=(peer, sub),
                device_id_type=MESH,
            ).start()

        for peer in peers:
            send(peer)
        dst[pl.ds(me, 1)] = src[pl.ds(me, 1)]
        return pltpu.make_async_remote_copy(
            src.at[pl.ds(0, PEERS - 1)],
            dst.at[pl.ds(0, PEERS - 1)],
            a2a_send.at[which],
            a2a_recv.at[which],
            device_id=after,
            device_id_type=MESH,
        )

    first = all_to_all(picked, received, 0)
    for copy in halos[2:]:
        copy.start()

    def own_corner(t, carry):
        cols = pl.ds(pl.multiple_of(t * LANES, LANES), LANES)
        at = hex_nodes[:, cols] + RIM * LANES
        zero = jnp.zeros((8, LANES), F32)
        got = lane_lookup(
            [zero] * 3, lambda c, r: ext[c, r : r + 1, :], range(RIM, RIM + ROWS), at >> 7, at & (LANES - 1)
        )
        for c in range(3):
            corner[c * 8 : (c + 1) * 8, cols] = got[c]
        return carry

    lax.fori_loop(0, ELEMS // LANES, own_corner, 0)

    force[...] = jnp.zeros_like(force)
    tied_out[...] = jnp.zeros_like(tied_out)
    for copy in halos[:2]:
        copy.wait()

    def rim_corner(t, carry):
        cols = pl.ds(pl.multiple_of(t * LANES, LANES), LANES)
        at = hex_nodes[:, cols] + RIM * LANES
        got = lane_lookup(
            [corner[c * 8 : (c + 1) * 8, cols] for c in range(3)],
            lambda c, r: ext[c, r : r + 1, :],
            [*range(RIM), *range(RIM + ROWS, EXT)],
            at >> 7,
            at & (LANES - 1),
        )
        for c in range(3):
            corner[c * 8 : (c + 1) * 8, cols] = got[c]
        return carry

    lax.fori_loop(0, ELEMS // LANES, rim_corner, 0)

    def element_force(t, carry):
        cols = pl.ds(pl.multiple_of(t * CHUNK, CHUNK), CHUNK)
        factor = modulus[:, cols] * jnp.where(yielded[:, cols] == 1, PLASTIC, 1.0)
        element = (
            jnp.dot(stiffness[...], corner[:, cols], precision=lax.Precision.HIGHEST, preferred_element_type=F32)
            * factor
        )
        at = hex_nodes[:, cols] + RIM * LANES
        row_at, lane_at = at >> 7, at & (LANES - 1)
        for k in range(8):
            force[...] += scatter_terms(
                EXT, row_at[k : k + 1], lane_at[k : k + 1], [element[c * 8 + k : c * 8 + k + 1] for c in range(3)]
            )
        return carry

    first.wait_recv()
    table[...] = jnp.transpose(received[...])
    slot = fine_slot[...]
    row_at, lane_at = slot & (CAP - 1), slot >> 5
    zero = jnp.zeros((8, LANES), F32)

    def lookup(rows, lanes):
        return lane_lookup(
            [zero] * 3, lambda c, r: table[c * CAP + r : c * CAP + r + 1, :], range(CAP), rows, lanes
        )

    def ends_first(x):
        return jnp.concatenate([x[:4], x[ROWS - 4 :]], axis=0)

    end_block = lookup(ends_first(row_at), ends_first(lane_at))
    for c in range(3):
        tied_out[0, 3 + c : 4 + c, :] = end_block[c][:1]
        tied_out[1, c : c + 1, :] = end_block[c][7:]
    ties = [to(before, tied_out.at[0], tied_in.at[1], 6), to(after, tied_out.at[1], tied_in.at[0], 7)]
    for copy in ties:
        copy.start()
    blocks = [
        lookup(row_at[4 + b * 8 : 12 + b * 8], lane_at[4 + b * 8 : 12 + b * 8]) for b in range(ROWS // 8 - 1)
    ]
    attached = [
        jnp.concatenate([end_block[c][:4]] + [b[c] for b in blocks] + [end_block[c][4:]], axis=0) for c in range(3)
    ]

    lane = lax.broadcasted_iota(jnp.int32, (ROWS, LANES), 1)

    def shifted(x):
        right = pltpu.roll(x, 1, 1)
        left = pltpu.roll(x, LANES - 1, 1)
        prev = jnp.where(lane == 0, pltpu.roll(right, 1, 0), right)
        nxt = jnp.where(lane == LANES - 1, pltpu.roll(left, ROWS - 1, 0), left)
        return prev, nxt

    pos = [pos_out[c] for c in range(3)]
    vel = [vel_out[c] for c in range(3)]
    total = [jnp.zeros((ROWS, LANES), F32) for _ in range(3)]
    im, st, tie = fine_inv_mass[...], fine_stiff[...], tie_stiff[...]
    first_rows = [x[:1] for x in pos + vel + [im, st, tie] + attached]
    last_rows = [x[ROWS - 1 :] for x in pos + vel + [im, st, tie] + attached]
    substeps(pos, vel, total, shifted, attached, im, st, tie)

    sub_row = lax.broadcasted_iota(jnp.int32, (ROWS, LANES), 0)
    at_head = (sub_row == 0) & (lane < EDGE)
    at_tail = (sub_row == ROWS - 1) & (lane >= LANES - EDGE)
    at_ends = at_head | at_tail

    def tie_force(sum_of_pos):
        return [tie * (sum_of_pos[c] * (1.0 / SUBSTEPS) - attached[c]) for c in range(3)]

    pull = [jnp.where(at_ends, 0.0, p) for p in tie_force(total)]
    sums = None
    for q in range(0, ROWS, 4):
        term = scatter_terms(CAP, flat(row_at, q), flat(lane_at, q), [flat(p, q) for p in pull])
        sums = term if sums is None else sums + term

    lax.fori_loop(0, 1, element_force, 0)
    for copy in halos[2:]:
        copy.wait()
    strip_lane = lax.broadcasted_iota(jnp.int32, (1, LANES), 1)
    starts = (me == 0) & (sub == 0)
    ends = (me == PEERS - 1) & (sub == n_sub - 1)

    def head(row, ghost):
        ghost = jnp.where(starts, 0.0, pltpu.roll(ghost, EDGE, 1))
        return jnp.where(strip_lane < EDGE, ghost, pltpu.roll(row, EDGE, 1))

    def tail(row, ghost):
        ghost = jnp.where(ends, 0.0, pltpu.roll(ghost, LANES - EDGE, 1))
        return jnp.where(strip_lane >= LANES - EDGE, ghost, pltpu.roll(row, LANES - EDGE, 1))

    heads = [head(r, edge_in[0, i : i + 1, :]) for i, r in enumerate(first_rows[:9])]
    tails = [tail(r, edge_in[1, i : i + 1, :]) for i, r in enumerate(last_rows[:9])]
    blank = jnp.zeros((2, LANES), F32)

    def strip(picks):
        return jnp.concatenate([heads[i] for i in picks] + [tails[i] for i in picks] + [blank], axis=0)

    strip_pos, strip_vel, strip_total = [strip((0, 1, 2))], [strip((3, 4, 5))], [jnp.zeros((8, LANES), F32)]
    strip_im, strip_st, strip_tie = strip((6, 6, 6)), strip((7, 7, 7)), strip((8, 8, 8))
    own_tied = jnp.concatenate(
        [pltpu.roll(x, EDGE, 1) for x in first_rows[9:]] + [pltpu.roll(x, LANES - EDGE, 1) for x in last_rows[9:]] + [blank],
        axis=0,
    )
    strip_row = lax.broadcasted_iota(jnp.int32, (8, LANES), 0)
    ghost_lane = lax.broadcasted_iota(jnp.int32, (8, LANES), 1)
    beyond = (starts & (strip_row < 3)) | (ends & (strip_row >= 3))
    from_before = (strip_row < 3) & (ghost_lane < EDGE)
    from_after = (strip_row >= 3) & (ghost_lane >= LANES - EDGE)
    for copy in ties:
        copy.wait()
    strip_tied = jnp.where(from_before, pltpu.roll(tied_in[0], EDGE, 1), own_tied)
    strip_tied = jnp.where(from_after, pltpu.roll(tied_in[1], LANES - EDGE, 1), strip_tied)
    strip_tied = jnp.where(beyond & (from_before | from_after), 0.0, strip_tied)
    substeps(
        strip_pos,
        strip_vel,
        strip_total,
        lambda x: (pltpu.roll(x, 1, 1), pltpu.roll(x, LANES - 1, 1)),
        [strip_tied],
        strip_im,
        strip_st,
        strip_tie,
    )

    def put_ends(whole, strips):
        forward = pltpu.roll(strips, LANES - EDGE, 1)
        back = pltpu.roll(strips, EDGE, 1)
        out = []
        for c in range(3):
            x = jnp.where(at_head, jnp.broadcast_to(forward[c : c + 1], (ROWS, LANES)), whole[c])
            out.append(jnp.where(at_tail, jnp.broadcast_to(back[3 + c : 4 + c], (ROWS, LANES)), x))
        return out

    pos = put_ends(pos, strip_pos[0])
    vel = put_ends(vel, strip_vel[0])
    total = put_ends(total, strip_total[0])
    end_pull = [jnp.where(at_ends, p, 0.0) for p in tie_force(total)]
    ends_of = lambda x: jnp.concatenate([x[:1], x[ROWS - 1 :]], axis=1)
    sums = sums + scatter_terms(CAP, ends_of(row_at), ends_of(lane_at), [ends_of(p) for p in end_pull])
    outgoing[...] = by_slot(joined(sums, CAP))
    second = all_to_all(outgoing, returned, 1)
    lax.fori_loop(1, 4, element_force, 0)
    for c in range(3):
        ext_force = force[2 * c * EXT : (2 * c + 1) * EXT, :] + force[(2 * c + 1) * EXT : (2 * c + 2) * EXT, :]
        force[2 * c * EXT : (2 * c + 1) * EXT, :] = ext_force
        force_in[2, c] = ext_force[:RIM]
        force_in[3, c] = ext_force[RIM + ROWS :]
    rims = [
        to(before, force_in.at[2], force_in.at[1], 4),
        to(after, force_in.at[3], force_in.at[0], 5),
    ]
    for copy in rims:
        copy.start()


    for q in range(ROWS):
        cols = slice(q * LANES, (q + 1) * LANES)
        pos_flat[:, cols] = jnp.concatenate([x[q : q + 1] for x in pos], axis=0)
        vel_flat[:, cols] = jnp.concatenate([x[q : q + 1] for x in vel], axis=0)
    for copy in rims:
        copy.wait()
    for c in range(3):
        own = force[2 * c * EXT + RIM : 2 * c * EXT + RIM + ROWS, :]
        internal[c, :RIM] = own[:RIM] + force_in[0, c]
        internal[c, RIM : ROWS - RIM] = own[RIM : ROWS - RIM]
        internal[c, ROWS - RIM :] = own[ROWS - RIM :] + force_in[1, c]
    first.wait_send()
    second.wait()


def update_kernel(
    disp, velo, inv_mass, send_slots, returned, internal, pos, vel, disp_new, velo_new, pos_out, vel_out, sem
):
    out = [pltpu.make_async_copy(pos, pos_out, sem.at[0]), pltpu.make_async_copy(vel, vel_out, sem.at[1])]
    for copy in out:
        copy.start()
    slot_at = send_slots[...]
    back = jnp.transpose(returned[...])
    back = [back[c * CAP : (c + 1) * CAP] for c in range(3)]
    row_at, lane_at = slot_at >> 7, slot_at & (LANES - 1)
    sums = None
    for q in range(0, CAP, 4):
        term = scatter_terms(ROWS, flat(row_at, q), flat(lane_at, q), [flat(b, q) for b in back])
        sums = term if sums is None else sums + term
    change = [inv_mass[...] * (coupling - internal[c]) for c, coupling in enumerate(joined(sums, ROWS))]
    for q in range(ROWS):
        cols = slice(q * LANES, (q + 1) * LANES)

        def three(x):
            return jnp.concatenate([x(c) for c in range(3)], axis=0)

        v = velo[:, cols] + DT_COARSE * three(lambda c: change[c][q : q + 1])
        velo_new[:, cols] = v
        disp_new[:, cols] = disp[:, cols] + DT_COARSE * v
    for copy in out:
        copy.wait()


def on_device(
    disp,
    velo,
    inv_mass,
    hex_nodes,
    modulus,
    yielded,
    stiffness,
    send_slots,
    fine_slot,
    fine_disp,
    fine_velo,
    fine_inv_mass,
    fine_stiff,
    tie_stiff,
):
    vmem = pl.BlockSpec(memory_space=pltpu.VMEM)
    chain = jax.ShapeDtypeStruct((3, ROWS, LANES), F32)
    flat_shape = jax.ShapeDtypeStruct(disp.shape, F32)
    rows = lambda x: x.reshape(ROWS, LANES)
    line = lambda x: x.reshape(1, ELEMS)
    buffer = lambda *shape: pltpu.VMEM(shape, F32)
    slots = send_slots.T
    loaded = (
        disp,
        slots,
        fine_disp,
        fine_velo,
        rows(fine_inv_mass),
        rows(fine_stiff),
        rows(tie_stiff),
        hex_nodes,
        rows(fine_slot),
        line(modulus),
        line(yielded),
        stiffness,
    )
    returned, internal, pos, vel = pl.pallas_call(
        exchange_kernel,
        out_shape=(jax.ShapeDtypeStruct((PEERS, LANES), F32), chain, flat_shape, flat_shape),
        in_specs=[pl.BlockSpec(memory_space=pltpu.HBM)] * 12,
        out_specs=(vmem,) * 4,
        scratch_shapes=[
            *[pltpu.VMEM(x.shape, x.dtype) for x in loaded],
            buffer(3, ROWS, LANES),
            buffer(3, ROWS, LANES),
            buffer(3, EXT, LANES),
            buffer(24, ELEMS),
            buffer(6 * EXT, LANES),
            buffer(4, 3, RIM, LANES),
            buffer(PEERS, LANES),
            buffer(PEERS, LANES),
            buffer(LANES, PEERS),
            buffer(PEERS, LANES),
            buffer(2, 16, LANES),
            buffer(2, 16, LANES),
            buffer(2, 8, LANES),
            buffer(2, 8, LANES),
            pltpu.SemaphoreType.DMA((2,)),
            pltpu.SemaphoreType.DMA((2,)),
            pltpu.SemaphoreType.DMA((8,)),
            pltpu.SemaphoreType.DMA((8,)),
            pltpu.SemaphoreType.DMA((len(loaded),)),
        ],
        compiler_params=pltpu.CompilerParams(
            collective_id=0, has_side_effects=True, vmem_limit_bytes=32 * 1024 * 1024
        ),
        name="exchange",
    )(*[pltpu.with_memory_space_constraint(x, pltpu.HBM) for x in loaded])
    return pl.pallas_call(
        update_kernel,
        out_shape=(flat_shape,) * 4,
        in_specs=[vmem] * 8,
        out_specs=(vmem, vmem, pl.BlockSpec(memory_space=pl.ANY), pl.BlockSpec(memory_space=pl.ANY)),
        scratch_shapes=[pltpu.SemaphoreType.DMA((2,))],
        compiler_params=pltpu.CompilerParams(vmem_limit_bytes=32 * 1024 * 1024),
        name="update",
    )(disp, velo, rows(inv_mass), slots, returned, internal, pos, vel)


def solution(mesh):
    placed = (
        P(None, ("mesh", "sub")),
        P(None, ("mesh", "sub")),
        P(("mesh", "sub")),
        P(None, ("mesh", "sub")),
        P(("mesh", "sub")),
        P(("mesh", "sub")),
        P(),
        P(("mesh", "sub"), None),
        P(("mesh", "sub")),
        P(None, ("mesh", "sub")),
        P(None, ("mesh", "sub")),
        P(("mesh", "sub")),
        P(("mesh", "sub")),
        P(("mesh", "sub")),
    )
    return jax.shard_map(
        on_device,
        mesh=mesh,
        in_specs=placed,
        out_specs=(
            P(None, ("mesh", "sub")),
            P(None, ("mesh", "sub")),
            P(None, ("mesh", "sub")),
            P(None, ("mesh", "sub")),
        ),
        check_vma=False,
    )
```
